512 devices in a mesh: dp: 256 (over z, y_hi, x, core), sub: 2 (over y_lo).
Axes of the slice: x: 4, y: 4 (y_hi: 2, y_lo: 2; y = y_hi * 2 + y_lo), z: 16, core: 2. Of those that a mesh axis runs over, the one named last changes fastest.
Arguments:
- photo_vectors: bfloat16 [131072, 1024], P(('dp', 'sub')), may hold values from -40 to 40
- caption_vectors: bfloat16 [131072, 1024], P(('dp', 'sub')), may hold values from -40 to 40
- inverse_heat_factor: float32 [1], replicated, may hold values from 1 to 4
Outputs:
- picture_gradient: float32 [131072, 1024], P(('dp', 'sub'))
- text_grad: float32 [131072, 1024], P(('dp', 'sub'))
The draws below stay inside these ranges and needn't reach their ends.
All inputs are finite; a program needn't handle non-finite values.
Results may differ from the reference program's by a relative error of at most 0.002.
Values may be sent and summed in bfloat16 or wider, within the bound.
A program may use at most 64 MiB of HBM per device.

```python
import math
import jax
import jax.numpy as jnp
from jax import lax

FEATURE_COUNT = 1024
TOK_DEV = 256
BAND = 4
TOKENS = 131072
N_DP = 256
N_SUB = 2


def draw_photo_vectors(key, part):
    key = jax.random.fold_in(key, 11)
    first_key = jax.random.fold_in(key, 0)
    own = jnp.clip(jax.random.normal(first_key, (TOKENS, FEATURE_COUNT), jnp.float32), -4.5, 4.5)
    result = own
    return result.astype(jnp.bfloat16)


def draw_caption_vectors(key, part):
    key = jax.random.fold_in(key, 23)
    first_key = jax.random.fold_in(key, 0)
    own = jnp.clip(jax.random.normal(first_key, (TOKENS, FEATURE_COUNT), jnp.float32), -4.5, 4.5)
    result = own
    return result.astype(jnp.bfloat16)


def setup_inputs(seed: int = 0) -> dict:
    streams_of = jax.random.split(jax.random.key(seed), 4)
    return {
        "photo_vectors": draw_photo_vectors(jax.random.fold_in(streams_of[3], 71), 0),
        "caption_vectors": draw_caption_vectors(jax.random.fold_in(streams_of[3], 71), 0),
        "inverse_heat_factor": jnp.clip(jnp.exp(jax.random.uniform(streams_of[2], (1,), jnp.float32, math.log(1.0), math.log(4.0))), 1.0, 4.0),
    }


def reference(photo_vectors, caption_vectors, inverse_heat_factor):
    block_rows = TOK_DEV * N_SUB
    count = N_DP
    img = photo_vectors.reshape(count, block_rows, FEATURE_COUNT)
    txt = caption_vectors.reshape(count, block_rows, FEATURE_COUNT)
    similarity_multiplier = inverse_heat_factor[0] * (1.0 / math.sqrt(FEATURE_COUNT))
    steps = jnp.arange(BAND).astype(jnp.int32)

    def band_index(b):
        return ((b + steps) % count).astype(jnp.int32)

    def logits(b):
        band_text = txt[band_index(b)].reshape(BAND * block_rows, FEATURE_COUNT)
        return (similarity_multiplier * jnp.dot(img[b], band_text.T, preferred_element_type=jnp.float32), band_text)

    def first(b):
        z, band_text = logits(b)
        return (jax.nn.logsumexp(z, axis=1), jax.nn.logsumexp(z.reshape(block_rows, BAND, block_rows), axis=0))
    row_lse, col_parts = lax.map(first, jnp.arange(count).astype(jnp.int32))
    rolled = jnp.stack([jnp.roll(col_parts[:, j], j, axis=0) for j in range(BAND)], 0)
    col_lse = jax.nn.logsumexp(rolled, axis=0)
    diag_mask = jnp.arange(BAND * block_rows)[None, :] == jnp.arange(block_rows)[:, None]

    def second(carry, b):
        z, band_text = logits(b)
        idx = band_index(b)
        band_lse = col_lse[idx].reshape(BAND * block_rows)
        weight = jnp.exp(z - row_lse[b][:, None]) + jnp.exp(z - band_lse[None, :])
        weight = weight - 2.0 * diag_mask.astype(weight.dtype)
        weight = (0.5 * similarity_multiplier * weight).astype(jnp.bfloat16)
        grad_rows = jnp.dot(weight, band_text, preferred_element_type=jnp.float32)
        parts = jnp.dot(weight.T, img[b], preferred_element_type=jnp.float32).reshape(BAND, block_rows, FEATURE_COUNT)
        carry = carry.at[idx].add(parts)
        return (carry, grad_rows)
    start = jnp.zeros((count, block_rows, FEATURE_COUNT), jnp.float32)
    text_sum, photo_sample_count = lax.scan(second, start, jnp.arange(count).astype(jnp.int32))
    return (photo_sample_count.reshape(TOKENS, FEATURE_COUNT), text_sum.reshape(TOKENS, FEATURE_COUNT))
```

```python
import math

import jax
import jax.numpy as jnp
from jax import lax
from jax.experimental import pallas as pl
from jax.experimental.pallas import tpu as pltpu
from jax.sharding import PartitionSpec as P

MESH = pl.DeviceIdType.MESH
PARTS = 4
GPARTS = 2

R_SIB = 0
R_T0 = R_SIB + PARTS
R_T2 = R_T0 + 1
R_T3 = R_T2 + PARTS
R_P0 = R_T3 + 1
R_P1 = R_P0 + 1
R_STAT = R_P1 + PARTS
R_GSIB = R_STAT + 8
R_GT2 = R_GSIB + GPARTS
R_GT0 = R_GT2 + 1
R_GTX = R_GT0 + 1
R_GB = R_GTX + 1
N_SEM = R_GB + 2 * GPARTS

S_SIB, S_OTHER, S_NEXT, S_PREV, S_NEXT_X, S_PREV_X = 0, 1, 2, 4, 6, 7


def nt(a, b):
    return lax.dot_general(a, b, (((1,), (1,)), ((), ())), preferred_element_type=jnp.float32)


def tn(a, b):
    return lax.dot_general(a, b, (((0,), (0,)), ((), ())), preferred_element_type=jnp.float32)


def nn(a, b):
    return lax.dot_general(a, b, (((1,), (0,)), ((), ())), preferred_element_type=jnp.float32)


def lse_down(z):
    top = jnp.max(z, axis=0, keepdims=True)
    return top + jnp.log(jnp.sum(jnp.exp(z - top), axis=0, keepdims=True))


def lse_along(z):
    top = jnp.max(z, axis=1, keepdims=True)
    lse = top + jnp.log(jnp.sum(jnp.exp(z - top), axis=1, keepdims=True))
    return jnp.transpose(jnp.broadcast_to(lse, (z.shape[0], 128)))[0:1]


def joined(*parts):
    top = parts[0]
    for part in parts[1:]:
        top = jnp.maximum(top, part)
    total = jnp.exp(parts[0] - top)
    for part in parts[1:]:
        total = total + jnp.exp(part - top)
    return top + jnp.log(total)


def upright(row):
    return jnp.transpose(jnp.broadcast_to(row, (128, row.shape[1])))[:, 0:1]


def kernel(n_dp, heat, im, tx, pg, tg, iall, iprev, tall, z, w, stat, stats, stage, gsib, gt2, gt0, gtx, gb,
           send_sem, recv_sem):
    rows, depth = im.shape
    b = lax.axis_index("dp")
    s = lax.axis_index("sub")
    core = lax.rem(b, 2)
    chip = b // 2
    chips = n_dp // 2

    def level(c):
        return lax.rem(c // 4, 2)

    def at(step, k, flip):
        c = lax.rem(chip + (chips + step), chips)
        lane = lax.rem(s + level(chip) + level(c) + flip, 2)
        return (c * 2 + k, lane)

    scale = heat[0] * (1.0 / math.sqrt(depth))
    part = rows // PARTS
    gpart = rows // GPARTS
    own = slice(0, rows)
    sib = slice(rows, 2 * rows)

    def piece(p):
        return pl.ds(p * part, part)

    def gpiece(p):
        return pl.ds(p * gpart, gpart)

    def text(t):
        return pl.ds(t * rows, rows)

    def run(k):
        sent = []

        def send(src, dst, index, to):
            copy = pltpu.make_async_remote_copy(
                src_ref=src, dst_ref=dst, send_sem=send_sem.at[len(sent)], recv_sem=recv_sem.at[index],
                device_id=to, device_id_type=MESH)
            copy.start()
            sent.append(copy)

        def arrived(dst, index):
            pltpu.make_async_remote_copy(
                src_ref=dst, dst_ref=dst, send_sem=send_sem.at[0], recv_sem=recv_sem.at[index],
                device_id=sibling, device_id_type=MESH).wait_recv()

        sibling = at(0, k, 1)
        other = at(0, 1 - k, 0)
        partners = [sibling, other, at(1, 0, 0), at(1, 1, 0), at(-1, 0, 0), at(-1, 1, 0)]
        if k == 1:
            partners += [at(1, 1, 1), at(-1, 1, 1)]
        barrier = pltpu.get_barrier_semaphore()
        for partner in partners:
            pl.semaphore_signal(barrier, inc=1, device_id=partner, device_id_type=MESH)
        pl.semaphore_wait(barrier, len(partners))

        send(tx, tall.at[text(k)], R_T0, other)
        if k == 0:
            for p in range(PARTS):
                send(tx.at[piece(p)], tall.at[pl.ds(2 * rows + p * part, part)], R_T2 + p, at(-1, 0, 0))
            for p in range(PARTS):
                send(im.at[piece(p)], iall.at[pl.ds(rows + p * part, part)], R_SIB + p, sibling)
        else:
            for p in range(PARTS):
                send(im.at[piece(p)], iall.at[pl.ds(rows + p * part, part)], R_SIB + p, sibling)
            send(im, iprev.at[pl.ds(0, rows)], R_P0, at(1, 1, 0))
            send(tx, tall.at[text(3)], R_T3, at(-1, 0, 0))

        iall[own, :] = im[...]
        tall[text(k), :] = tx[...]

        def logits(images, half, t, column):
            z[half * rows:(half + 1) * rows, column * rows:(column + 1) * rows] = scale * nt(
                images[half * rows:(half + 1) * rows, :], tall[text(t), :])

        stat[...] = jnp.zeros_like(stat)
        if k == 0:
            logits(iall, 0, 0, 0)
            arrived(tall.at[text(1)], R_T0)
            logits(iall, 0, 1, 1)
            for p in range(PARTS):
                piece_ref = tall.at[pl.ds(2 * rows + p * part, part)]
                arrived(piece_ref, R_T2 + p)
                send(piece_ref, piece_ref, R_T2 + p, other)
            logits(iall, 0, 2, 2)
            for p in range(PARTS):
                arrived(iall.at[pl.ds(rows + p * part, part)], R_SIB + p)
            for t in range(3):
                logits(iall, 1, t, t)
                stat[t:t + 1, :] = lse_down(z[:, t * rows:(t + 1) * rows])
            arrived(tall.at[text(3)], R_T3)
            for half in range(2):
                logits(iall, half, 3, 3)
            stat[3:4, :] = lse_down(z[:, 3 * rows:])
            for half in range(2):
                stat[4 + half:5 + half, :] = lse_along(z[half * rows:(half + 1) * rows, :])
        else:
            logits(iall, 0, 1, 3)
            arrived(tall.at[text(0)], R_T0)
            for p in range(PARTS):
                piece_ref = iall.at[pl.ds(rows + p * part, part)]
                arrived(piece_ref, R_SIB + p)
                send(piece_ref, iprev.at[pl.ds(rows + p * part, part)], R_P1 + p, at(1, 1, 0))
            logits(iall, 1, 1, 3)
            for half in range(2):
                stat[4 + half:5 + half, :] = lse_along(z[half * rows:(half + 1) * rows, 3 * rows:])
            arrived(iprev.at[pl.ds(0, rows)], R_P0)
            logits(iprev, 0, 0, 0)
            logits(iprev, 0, 1, 1)
            for p in range(PARTS):
                arrived(tall.at[pl.ds(2 * rows + p * part, part)], R_T2 + p)
            logits(iprev, 0, 2, 2)
            stat[6:7, :] = lse_along(z[own, :3 * rows])
            for p in range(PARTS):
                arrived(iprev.at[pl.ds(rows + p * part, part)], R_P1 + p)
            for t in range(3):
                logits(iprev, 1, t, t)
            stat[7:8, :] = lse_along(z[sib, :3 * rows])
            stat[0:1, :] = lse_down(z[:, :rows])
            stat[1:2, :] = joined(lse_down(z[:, rows:2 * rows]), lse_down(z[:, 3 * rows:]))
            stat[2:3, :] = lse_down(z[:, 2 * rows:3 * rows])

        send(stat, stats.at[S_SIB], R_STAT + S_SIB, sibling)
        send(stat, stats.at[S_PREV + k], R_STAT + S_PREV + k, at(1, 0, 0))
        send(stat, stats.at[S_PREV + k], R_STAT + S_PREV + k, at(1, 1, 0))
        send(stat, stats.at[S_NEXT + k], R_STAT + S_NEXT + k, at(-1, 0, 0))
        send(stat, stats.at[S_NEXT + k], R_STAT + S_NEXT + k, at(-1, 1, 0))
        if k == 1:
            send(stat, stats.at[S_PREV_X], R_STAT + S_PREV_X, at(1, 1, 1))
            send(stat, stats.at[S_NEXT_X], R_STAT + S_NEXT_X, at(-1, 1, 1))
        send(stat, stats.at[S_OTHER], R_STAT + S_OTHER, other)
        for slot in range(6 if k == 0 else 8):
            arrived(stats.at[slot], R_STAT + slot)

        def line(slot, row):
            return stats[slot, row:row + 1, :]

        def mine(row):
            return stat[row:row + 1, :]

        col = [
            joined(mine(0), line(S_OTHER, 0), line(S_PREV, 2), line(S_PREV + 1, 2)),
            joined(mine(1), line(S_OTHER, 1), line(S_PREV, 3)),
            joined(mine(2), line(S_OTHER, 2), line(S_NEXT, 0), line(S_NEXT + 1, 0)),
        ]
        if k == 0:
            col.append(joined(mine(3), line(S_NEXT, 1), line(S_NEXT + 1, 1)))
            row_a = [upright(joined(mine(4 + h), line(S_SIB, 5 - h))) for h in range(2)]
        else:
            row_a = [
                upright(joined(mine(4 + h), line(S_SIB, 5 - h), line(S_NEXT + 1, 6 + h), line(S_NEXT_X, 7 - h)))
                for h in range(2)]
            row_b = [
                upright(joined(mine(6 + h), line(S_SIB, 7 - h), line(S_PREV + 1, 4 + h), line(S_PREV_X, 5 - h)))
                for h in range(2)]

        def weigh(half, column, row_lse, col_lse, diagonal):
            at_rows = slice(half * rows, (half + 1) * rows)
            at_cols = slice(column * rows, (column + 1) * rows)
            block = z[at_rows, at_cols]
            weight = jnp.exp(block - row_lse) + jnp.exp(block - col_lse)
            if diagonal:
                i = lax.broadcasted_iota(jnp.int32, (rows, rows), 0)
                j = lax.broadcasted_iota(jnp.int32, (rows, rows), 1)
                weight = weight - 2.0 * (i == j).astype(jnp.float32)
            w[at_rows, at_cols] = (0.5 * scale * weight).astype(jnp.bfloat16)

        def columns(column):
            return slice(column * rows, (column + 1) * rows)

        b16 = jnp.bfloat16
        f32 = jnp.float32
        if k == 0:
            for half in range(2):
                weigh(half, 3, row_a[half], col[3], False)
            stage[0] = tn(w[:, columns(3)], iall[...]).astype(b16)
            send(stage.at[0], gtx, R_GTX, at(1, 1, 0))
            for half in range(2):
                weigh(half, 2, row_a[half], col[2], False)
            part_2 = tn(w[:, columns(2)], iall[...])
            arrived(gt2, R_GT2)
            stage[1] = (part_2 + gt2[...].astype(f32)).astype(b16)
            send(stage.at[1], gtx, R_GTX, at(1, 0, 0))
            for t in range(2):
                weigh(1, t, row_a[1], col[t], False)
            stage[2] = nn(w[sib, :], tall[...]).astype(b16)
            for p in range(GPARTS):
                send(stage.at[2, gpiece(p)], gsib.at[gpiece(p)], R_GSIB + p, sibling)
            for t in range(2):
                weigh(0, t, row_a[0], col[t], t == 0)
            stage[3] = tn(w[:, columns(1)], iall[...]).astype(b16)
            send(stage.at[3], gt0, R_GT0, other)
            tg[...] = tn(w[:, columns(0)], iall[...])
            pg[...] = nn(w[own, :], tall[...])
            arrived(gt0, R_GT0)
            tg[...] += gt0[...].astype(f32)
            for p in range(GPARTS):
                arrived(gsib.at[gpiece(p)], R_GSIB + p)
                pg[gpiece(p), :] += gsib[gpiece(p), :].astype(f32)
            arrived(gtx, R_GTX)
            tg[...] += gtx[...].astype(f32)
        else:
            for half in range(2):
                weigh(half, 2, row_b[half], col[2], False)
            stage[0] = tn(w[:, columns(2)], iprev[...]).astype(b16)
            send(stage.at[0], gt2, R_GT2, other)
            for half in (1, 0):
                for t in range(2):
                    weigh(half, t, row_b[half], col[t], False)
                stage[1 + half] = nn(w[half * rows:(half + 1) * rows, :3 * rows], tall[pl.ds(0, 3 * rows), :]).astype(b16)
                for p in range(GPARTS):
                    send(stage.at[1 + half, gpiece(p)], gb.at[half, gpiece(p)], R_GB + half * GPARTS + p, at(-1, 1, 0))
            stage[3] = tn(w[:, columns(0)], iprev[...]).astype(b16)
            send(stage.at[3], gt0, R_GT0, other)
            for half in range(2):
                weigh(half, 3, row_a[half], col[1], half == 0)
            pg[...] = nn(w[sib, columns(3)], tall[text(1), :])
            tg[...] = tn(w[:, columns(1)], iprev[...]) + tn(w[:, columns(3)], iall[...])
            for p in range(GPARTS):
                arrived(gb.at[1, gpiece(p)], R_GB + GPARTS + p)
                stage[4, gpiece(p), :] = (pg[gpiece(p), :] + gb[1, gpiece(p), :].astype(f32)).astype(b16)
                send(stage.at[4, gpiece(p)], gsib.at[gpiece(p)], R_GSIB + p, sibling)
            pg[...] = nn(w[own, columns(3)], tall[text(1), :])
            arrived(gt0, R_GT0)
            tg[...] += gt0[...].astype(f32)
            arrived(gtx, R_GTX)
            tg[...] += gtx[...].astype(f32)
            for p in range(GPARTS):
                arrived(gb.at[0, gpiece(p)], R_GB + p)
                pg[gpiece(p), :] += gb[0, gpiece(p), :].astype(f32)
            for p in range(GPARTS):
                arrived(gsib.at[gpiece(p)], R_GSIB + p)
                pg[gpiece(p), :] += gsib[gpiece(p), :].astype(f32)
        for copy in sent:
            copy.wait_send()

    @pl.when(core == 0)
    def _():
        run(0)

    @pl.when(core == 1)
    def _():
        run(1)


def local(photo_vectors, caption_vectors, inverse_heat_factor):
    rows, depth = photo_vectors.shape
    n_dp = lax.axis_size("dp")
    vmem = pl.BlockSpec(memory_space=pltpu.VMEM)
    bf16 = jnp.bfloat16
    block = pltpu.VMEM((rows, depth), bf16)

    def body(*refs):
        kernel(n_dp, *refs)

    return pl.pallas_call(
        body,
        out_shape=[jax.ShapeDtypeStruct((rows, depth), jnp.float32)] * 2,
        in_specs=[pl.BlockSpec(memory_space=pltpu.SMEM), vmem, vmem],
        out_specs=[vmem, vmem],
        scratch_shapes=[
            pltpu.VMEM((2 * rows, depth), bf16),
            pltpu.VMEM((2 * rows, depth), bf16),
            pltpu.VMEM((4 * rows, depth), bf16),
            pltpu.VMEM((2 * rows, 4 * rows), jnp.float32),
            pltpu.VMEM((2 * rows, 4 * rows), bf16),
            pltpu.VMEM((8, rows), jnp.float32),
            pltpu.VMEM((8, 8, rows), jnp.float32),
            pltpu.VMEM((5, rows, depth), bf16),
            block,
            block,
            block,
            block,
            pltpu.VMEM((2, rows, depth), bf16),
            pltpu.SemaphoreType.DMA((40,)),
            pltpu.SemaphoreType.DMA((N_SEM,)),
        ],
        compiler_params=pltpu.CompilerParams(
            collective_id=0, has_side_effects=True, vmem_limit_bytes=48 * 2**20),
        cost_estimate=pl.CostEstimate(
            flops=6 * 2 * rows * 4 * rows * depth, bytes_accessed=12 * rows * depth,
            transcendentals=4 * 8 * rows * rows),
        name="banded",
    )(inverse_heat_factor, photo_vectors, caption_vectors)


def solution(mesh):
    in_specs = (P(("dp", "sub"), None), P(("dp", "sub"), None), P())
    out_specs = (P(("dp", "sub"), None), P(("dp", "sub"), None))
    return jax.shard_map(local, mesh=mesh, in_specs=in_specs, out_specs=out_specs, check_vma=False)
```

```python
import math

import jax
import jax.numpy as jnp
from jax import lax
from jax.experimental import pallas as pl
from jax.experimental.pallas import tpu as pltpu
from jax.sharding import PartitionSpec as P

MESH = pl.DeviceIdType.MESH
PARTS = 4
GPARTS = 2

R_SIB = 0
R_T0 = R_SIB + PARTS
R_T2 = R_T0 + 1
R_T3 = R_T2 + PARTS
R_P0 = R_T3 + PARTS
R_P1 = R_P0 + 1
R_STAT = R_P1 + PARTS
R_GSIB = R_STAT + 8
R_GT2 = R_GSIB + GPARTS
R_GT0 = R_GT2 + 1
R_GTX = R_GT0 + 1
R_GB = R_GTX + 1
N_SEM = R_GB + 2 * GPARTS

S_SIB, S_OTHER, S_NEXT, S_PREV, S_NEXT_X, S_PREV_X = 0, 1, 2, 4, 6, 7


def nt(a, b):
    return lax.dot_general(a, b, (((1,), (1,)), ((), ())), preferred_element_type=jnp.float32)


def tn(a, b):
    return lax.dot_general(a, b, (((0,), (0,)), ((), ())), preferred_element_type=jnp.float32)


def nn(a, b):
    return lax.dot_general(a, b, (((1,), (0,)), ((), ())), preferred_element_type=jnp.float32)


def lse_down(z):
    top = jnp.max(z, axis=0, keepdims=True)
    return top + jnp.log(jnp.sum(jnp.exp(z - top), axis=0, keepdims=True))


def lse_along(z):
    top = jnp.max(z, axis=1, keepdims=True)
    lse = top + jnp.log(jnp.sum(jnp.exp(z - top), axis=1, keepdims=True))
    return jnp.transpose(jnp.broadcast_to(lse, (z.shape[0], 128)))[0:1]


def joined(*parts):
    top = parts[0]
    for part in parts[1:]:
        top = jnp.maximum(top, part)
    total = jnp.exp(parts[0] - top)
    for part in parts[1:]:
        total = total + jnp.exp(part - top)
    return top + jnp.log(total)


def upright(row):
    return jnp.transpose(jnp.broadcast_to(row, (128, row.shape[1])))[:, 0:1]


def kernel(n_dp, heat, im, tx, pg, tg, gsib, gtx, iall, iprev, tall, z, w, stat, stats, stage, gt2, gt0, gb,
           send_sem, recv_sem, load_sem):
    rows, depth = im.shape
    b = lax.axis_index("dp")
    s = lax.axis_index("sub")
    core = lax.rem(b, 2)
    chip = b // 2
    chips = n_dp // 2

    def level(c):
        return lax.rem(c // 4, 2)

    def at(step, k, flip):
        c = lax.rem(chip + (chips + step), chips)
        lane = lax.rem(s + level(chip) + level(c) + flip, 2)
        return (c * 2 + k, lane)

    scale = heat[0] * (1.0 / math.sqrt(depth))
    part = rows // PARTS
    gpart = rows // GPARTS
    own = slice(0, rows)
    sib = slice(rows, 2 * rows)

    def piece(p):
        return pl.ds(p * part, part)

    def gpiece(p):
        return pl.ds(p * gpart, gpart)

    def text(t):
        return pl.ds(t * rows, rows)

    def run(k):
        sent = []
        sent_early = []

        def send(src, dst, index, to):
            copy = pltpu.make_async_remote_copy(
                src_ref=src, dst_ref=dst, send_sem=send_sem.at[len(sent)], recv_sem=recv_sem.at[index],
                device_id=to, device_id_type=MESH)
            copy.start()
            sent.append(copy)

        def arrived(dst, index):
            pltpu.make_async_remote_copy(
                src_ref=dst, dst_ref=dst, send_sem=send_sem.at[0], recv_sem=recv_sem.at[index],
                device_id=sibling, device_id_type=MESH).wait_recv()

        sibling = at(0, k, 1)
        other = at(0, 1 - k, 0)
        partners = [sibling, other, at(1, 0, 0), at(1, 1, 0), at(-1, 0, 0), at(-1, 1, 0)]
        barrier = pltpu.get_barrier_semaphore()
        for partner in partners:
            pl.semaphore_signal(barrier, inc=1, device_id=partner, device_id_type=MESH)
        load_text = pltpu.make_async_copy(tx, tall.at[text(k)], load_sem.at[0])
        load_image = pltpu.make_async_copy(im, iall.at[pl.ds(0, rows)], load_sem.at[1])
        load_text.start()
        load_image.start()

        def logits(images, half, t, column):
            z[half * rows:(half + 1) * rows, column * rows:(column + 1) * rows] = scale * nt(
                images[half * rows:(half + 1) * rows, :], tall[text(t), :])

        def block(half, first, last):
            return z[half * rows:(half + 1) * rows, first * rows:last * rows]

        stat[...] = jnp.zeros_like(stat)
        load_text.wait()
        load_image.wait()
        logits(iall, 0, k, 0 if k == 0 else 3)
        pl.semaphore_wait(barrier, len(partners))

        def send_sib(p):
            send(im.at[piece(p)], iall.at[pl.ds(rows + p * part, part)], R_SIB + p, sibling)

        if k == 0:
            for p in range(PARTS):
                send(tx.at[piece(p)], tall.at[pl.ds(2 * rows + p * part, part)], R_T2 + p, at(-1, 0, 0))
            send(tx, tall.at[text(0)], R_T0, other)
            send_sib(0)
            arrived(tall.at[text(1)], R_T0)
            logits(iall, 0, 1, 1)
            for p in range(PARTS):
                piece_ref = tall.at[pl.ds(2 * rows + p * part, part)]
                arrived(piece_ref, R_T2 + p)
                send(piece_ref, piece_ref, R_T2 + p, other)
                if p + 1 < PARTS:
                    send_sib(p + 1)
            logits(iall, 0, 2, 2)
            row_0 = lse_along(block(0, 0, 3))
            for p in range(PARTS):
                arrived(iall.at[pl.ds(rows + p * part, part)], R_SIB + p)
            for t in range(3):
                logits(iall, 1, t, t)
            for t in range(3):
                stat[t:t + 1, :] = lse_down(z[:, t * rows:(t + 1) * rows])
            row_1 = lse_along(block(1, 0, 3))
            for p in range(PARTS):
                arrived(tall.at[pl.ds(3 * rows + p * part, part)], R_T3 + p)
            for half in range(2):
                logits(iall, half, 3, 3)
            stat[3:4, :] = lse_down(z[:, 3 * rows:])
            stat[4:5, :] = joined(row_0, lse_along(block(0, 3, 4)))
            stat[5:6, :] = joined(row_1, lse_along(block(1, 3, 4)))
        else:
            def send_t3(p):
                send(tx.at[piece(p)], tall.at[pl.ds(3 * rows + p * part, part)], R_T3 + p, at(-1, 0, 0))

            for p in range(PARTS):
                send_sib(p)
            send(im, iprev.at[pl.ds(0, rows)], R_P0, at(1, 1, 0))
            send(tx, tall.at[text(1)], R_T0, other)
            send_t3(0)
            for p in range(PARTS):
                piece_ref = iall.at[pl.ds(rows + p * part, part)]
                arrived(piece_ref, R_SIB + p)
                send(piece_ref, iprev.at[pl.ds(rows + p * part, part)], R_P1 + p, at(1, 1, 0))
                if p + 1 < PARTS:
                    send_t3(p + 1)
            logits(iall, 1, 1, 3)
            for half in range(2):
                stat[4 + half:5 + half, :] = lse_along(block(half, 3, 4))
            col_a = lse_down(z[:, 3 * rows:])
            arrived(tall.at[text(0)], R_T0)
            arrived(iprev.at[pl.ds(0, rows)], R_P0)
            logits(iprev, 0, 0, 0)
            logits(iprev, 0, 1, 1)
            for p in range(PARTS):
                arrived(tall.at[pl.ds(2 * rows + p * part, part)], R_T2 + p)
            logits(iprev, 0, 2, 2)
            stat[6:7, :] = lse_along(block(0, 0, 3))
            col_b = [lse_down(block(0, t, t + 1)) for t in range(3)]
            col_b[1] = joined(col_b[1], col_a)
            for p in range(PARTS):
                arrived(iprev.at[pl.ds(rows + p * part, part)], R_P1 + p)
            for t in range(3):
                logits(iprev, 1, t, t)
            stat[7:8, :] = lse_along(block(1, 0, 3))
            for t in range(3):
                stat[t:t + 1, :] = joined(col_b[t], lse_down(block(1, t, t + 1)))

        if k == 1:
            send(stat, stats.at[S_PREV_X], R_STAT + S_PREV_X, at(1, 1, 1))
            send(stat, stats.at[S_NEXT_X], R_STAT + S_NEXT_X, at(-1, 1, 1))
        send(stat, stats.at[S_PREV + k], R_STAT + S_PREV + k, at(1, 1, 0))
        send(stat, stats.at[S_PREV + k], R_STAT + S_PREV + k, at(1, 0, 0))
        send(stat, stats.at[S_NEXT + k], R_STAT + S_NEXT + k, at(-1, 1, 0))
        send(stat, stats.at[S_NEXT + k], R_STAT + S_NEXT + k, at(-1, 0, 0))
        send(stat, stats.at[S_SIB], R_STAT + S_SIB, sibling)
        send(stat, stats.at[S_OTHER], R_STAT + S_OTHER, other)
        for slot in range(6 if k == 0 else 8):
            arrived(stats.at[slot], R_STAT + slot)

        def line(slot, row):
            return stats[slot, row:row + 1, :]

        def mine(row):
            return stat[row:row + 1, :]

        col = [
            joined(mine(0), line(S_OTHER, 0), line(S_PREV, 2), line(S_PREV + 1, 2)),
            joined(mine(1), line(S_OTHER, 1), line(S_PREV, 3)),
            joined(mine(2), line(S_OTHER, 2), line(S_NEXT, 0), line(S_NEXT + 1, 0)),
        ]
        if k == 0:
            col.append(joined(mine(3), line(S_NEXT, 1), line(S_NEXT + 1, 1)))
            row_a = [upright(joined(mine(4 + h), line(S_SIB, 5 - h))) for h in range(2)]
        else:
            row_a = [
                upright(joined(mine(4 + h), line(S_SIB, 5 - h), line(S_NEXT + 1, 6 + h), line(S_NEXT_X, 7 - h)))
                for h in range(2)]
            row_b = [
                upright(joined(mine(6 + h), line(S_SIB, 7 - h), line(S_PREV + 1, 4 + h), line(S_PREV_X, 5 - h)))
                for h in range(2)]

        def weigh(half, column, row_lse, col_lse, diagonal):
            at_rows = slice(half * rows, (half + 1) * rows)
            at_cols = slice(column * rows, (column + 1) * rows)
            block = z[at_rows, at_cols]
            weight = jnp.exp(block - row_lse) + jnp.exp(block - col_lse)
            if diagonal:
                i = lax.broadcasted_iota(jnp.int32, (rows, rows), 0)
                j = lax.broadcasted_iota(jnp.int32, (rows, rows), 1)
                weight = weight - 2.0 * (i == j).astype(jnp.float32)
            w[at_rows, at_cols] = (0.5 * scale * weight).astype(jnp.bfloat16)

        def columns(column):
            return slice(column * rows, (column + 1) * rows)

        b16 = jnp.bfloat16
        f32 = jnp.float32
        if k == 0:
            for half in range(2):
                weigh(half, 3, row_a[half], col[3], False)
            stage[0] = tn(w[:, columns(3)], iall[...]).astype(b16)
            send(stage.at[0], gtx, R_GTX, at(1, 1, 0))
            for t in range(3):
                weigh(1, t, row_a[1], col[t], False)
            stage[2] = nn(w[sib, :], tall[...]).astype(b16)
            for p in range(GPARTS):
                send(stage.at[2, gpiece(p)], gsib.at[gpiece(p)], R_GSIB + p, sibling)
            weigh(0, 2, row_a[0], col[2], False)
            part_2 = tn(w[:, columns(2)], iall[...])
            arrived(gt2, R_GT2)
            stage[1] = (part_2 + gt2[...].astype(f32)).astype(b16)
            send(stage.at[1], gtx, R_GTX, at(1, 0, 0))
            for t in range(2):
                weigh(0, t, row_a[0], col[t], t == 0)
            stage[3] = tn(w[:, columns(1)], iall[...]).astype(b16)
            send(stage.at[3], gt0, R_GT0, other)
            tg[...] = tn(w[:, columns(0)], iall[...])
            pg[...] = nn(w[own, :], tall[...])
            arrived(gt0, R_GT0)
            tg[...] += gt0[...].astype(f32)
            for p in range(GPARTS):
                arrived(gsib.at[gpiece(p)], R_GSIB + p)
            arrived(gtx, R_GTX)
        else:
            for t in range(3):
                weigh(1, t, row_b[1], col[t], False)
            stage[2] = nn(w[sib, :3 * rows], tall[pl.ds(0, 3 * rows), :]).astype(b16)
            first = len(sent)
            for p in range(GPARTS):
                send(stage.at[2, gpiece(p)], gb.at[1, gpiece(p)], R_GB + GPARTS + p, at(-1, 1, 0))
            weigh(0, 2, row_b[0], col[2], False)
            stage[0] = tn(w[:, columns(2)], iprev[...]).astype(b16)
            send(stage.at[0], gt2, R_GT2, other)
            for t in range(2):
                weigh(0, t, row_b[0], col[t], False)
            stage[1] = nn(w[own, :3 * rows], tall[pl.ds(0, 3 * rows), :]).astype(b16)
            stage[3] = tn(w[:, columns(0)], iprev[...]).astype(b16)
            send(stage.at[3], gt0, R_GT0, other)
            for half in range(2):
                weigh(half, 3, row_a[half], col[1], half == 0)
            pg[...] = nn(w[sib, columns(3)], tall[text(1), :])
            tg[...] = tn(w[:, columns(1)], iprev[...]) + tn(w[:, columns(3)], iall[...])
            for p in range(GPARTS):
                sent[first + p].wait_send()
                send(stage.at[1, gpiece(p)], gb.at[0, gpiece(p)], R_GB + p, at(-1, 1, 0))
            sent_early.extend(range(first, first + GPARTS))
            for p in range(GPARTS):
                arrived(gb.at[1, gpiece(p)], R_GB + GPARTS + p)
                stage[4, gpiece(p), :] = (pg[gpiece(p), :] + gb[1, gpiece(p), :].astype(f32)).astype(b16)
                send(stage.at[4, gpiece(p)], gsib.at[gpiece(p)], R_GSIB + p, sibling)
            pg[...] = nn(w[own, columns(3)], tall[text(1), :])
            arrived(gt0, R_GT0)
            tg[...] += gt0[...].astype(f32)
            for p in range(GPARTS):
                arrived(gb.at[0, gpiece(p)], R_GB + p)
                pg[gpiece(p), :] += gb[0, gpiece(p), :].astype(f32)
            arrived(gtx, R_GTX)
            for p in range(GPARTS):
                arrived(gsib.at[gpiece(p)], R_GSIB + p)
        for index, copy in enumerate(sent):
            if index not in sent_early:
                copy.wait_send()

    @pl.when(core == 0)
    def _():
        run(0)

    @pl.when(core == 1)
    def _():
        run(1)


def local(photo_vectors, caption_vectors, inverse_heat_factor):
    rows, depth = photo_vectors.shape
    n_dp = lax.axis_size("dp")
    vmem = pl.BlockSpec(memory_space=pltpu.VMEM)
    bf16 = jnp.bfloat16
    block = pltpu.VMEM((rows, depth), bf16)

    def body(*refs):
        kernel(n_dp, *refs)

    hbm = pl.BlockSpec(memory_space=pltpu.HBM)
    pg, tg, gsib, gtx = pl.pallas_call(
        body,
        out_shape=[jax.ShapeDtypeStruct((rows, depth), jnp.float32)] * 2
        + [jax.ShapeDtypeStruct((rows, depth), bf16)] * 2,
        in_specs=[pl.BlockSpec(memory_space=pltpu.SMEM), hbm, hbm],
        out_specs=[vmem] * 4,
        scratch_shapes=[
            pltpu.VMEM((2 * rows, depth), bf16),
            pltpu.VMEM((2 * rows, depth), bf16),
            pltpu.VMEM((4 * rows, depth), bf16),
            pltpu.VMEM((2 * rows, 4 * rows), jnp.float32),
            pltpu.VMEM((2 * rows, 4 * rows), bf16),
            pltpu.VMEM((8, rows), jnp.float32),
            pltpu.VMEM((8, 8, rows), jnp.float32),
            pltpu.VMEM((5, rows, depth), bf16),
            block,
            block,
            pltpu.VMEM((2, rows, depth), bf16),
            pltpu.SemaphoreType.DMA((40,)),
            pltpu.SemaphoreType.DMA((N_SEM,)),
            pltpu.SemaphoreType.DMA((2,)),
        ],
        compiler_params=pltpu.CompilerParams(
            collective_id=0, has_side_effects=True, vmem_limit_bytes=48 * 2**20),
        cost_estimate=pl.CostEstimate(
            flops=6 * 2 * rows * 4 * rows * depth, bytes_accessed=12 * rows * depth,
            transcendentals=4 * 8 * rows * rows),
        name="banded",
    )(inverse_heat_factor, pltpu.with_memory_space_constraint(photo_vectors, pltpu.HBM), pltpu.with_memory_space_constraint(caption_vectors, pltpu.HBM))
    return pg + gsib.astype(jnp.float32), tg + gtx.astype(jnp.float32)


def solution(mesh):
    in_specs = (P(("dp", "sub"), None), P(("dp", "sub"), None), P())
    out_specs = (P(("dp", "sub"), None), P(("dp", "sub"), None))
    return jax.shard_map(local, mesh=mesh, in_specs=in_specs, out_specs=out_specs, check_vma=False)
```

```python
import math

import jax
import jax.numpy as jnp
from jax import lax
from jax.experimental import pallas as pl
from jax.experimental.pallas import tpu as pltpu
from jax.sharding import PartitionSpec as P

MESH = pl.DeviceIdType.MESH
PARTS = 4
GPARTS = 2

R_SIB = 0
R_T0 = R_SIB + PARTS
R_T2 = R_T0 + 1
R_T3 = R_T2 + PARTS
R_P0 = R_T3 + PARTS
R_P1 = R_P0 + 1
R_STAT = R_P1 + PARTS
R_GSIB = R_STAT + 8
R_GT2 = R_GSIB + GPARTS
R_GT0 = R_GT2 + 1
R_GTX = R_GT0 + 1
R_GB = R_GTX + 1
N_SEM = R_GB + 2 * GPARTS

S_SIB, S_OTHER, S_NEXT, S_PREV, S_NEXT_X, S_PREV_X = 0, 1, 2, 4, 6, 7


def nt(a, b):
    return lax.dot_general(a, b, (((1,), (1,)), ((), ())), preferred_element_type=jnp.float32)


def tn(a, b):
    return lax.dot_general(a, b, (((0,), (0,)), ((), ())), preferred_element_type=jnp.float32)


def nn(a, b):
    return lax.dot_general(a, b, (((1,), (0,)), ((), ())), preferred_element_type=jnp.float32)


def lse_down(z):
    top = jnp.max(z, axis=0, keepdims=True)
    return top + jnp.log(jnp.sum(jnp.exp(z - top), axis=0, keepdims=True))


def lse_along(z):
    top = jnp.max(z, axis=1, keepdims=True)
    lse = top + jnp.log(jnp.sum(jnp.exp(z - top), axis=1, keepdims=True))
    return jnp.transpose(jnp.broadcast_to(lse, (z.shape[0], 128)))[0:1]


def joined(*parts):
    top = parts[0]
    for part in parts[1:]:
        top = jnp.maximum(top, part)
    total = jnp.exp(parts[0] - top)
    for part in parts[1:]:
        total = total + jnp.exp(part - top)
    return top + jnp.log(total)


def upright(row):
    return jnp.transpose(jnp.broadcast_to(row, (128, row.shape[1])))[:, 0:1]


def kernel(n_dp, heat, im, tx, pg, tg, gsib, gtx, iall, iprev, tall, z, w, stat, stats, stage, gt2, gt0, gb,
           send_sem, recv_sem, load_sem):
    rows, depth = im.shape
    b = lax.axis_index("dp")
    s = lax.axis_index("sub")
    core = lax.rem(b, 2)
    chip = b // 2
    chips = n_dp // 2

    def level(c):
        return lax.rem(c // 4, 2)

    near = {}
    for step in (-1, 0, 1):
        c = chip if step == 0 else lax.rem(chip + (chips + step), chips)
        near[step] = (c * 2, s if step == 0 else lax.rem(s + level(chip) + level(c), 2))

    def at(step, k, flip):
        first, lane = near[step]
        return (first + k, 1 - lane if flip else lane)

    scale = heat[0] * (1.0 / math.sqrt(depth))
    part = rows // PARTS
    gpart = rows // GPARTS
    own = slice(0, rows)
    sib = slice(rows, 2 * rows)

    def piece(p):
        return pl.ds(p * part, part)

    def gpiece(p):
        return pl.ds(p * gpart, gpart)

    def text(t):
        return pl.ds(t * rows, rows)

    def run(k):
        sent = []
        sent_early = []

        def send(src, dst, index, to):
            copy = pltpu.make_async_remote_copy(
                src_ref=src, dst_ref=dst, send_sem=send_sem.at[len(sent)], recv_sem=recv_sem.at[index],
                device_id=to, device_id_type=MESH)
            copy.start()
            sent.append(copy)

        def arrived(dst, index):
            pltpu.make_async_remote_copy(
                src_ref=dst, dst_ref=dst, send_sem=send_sem.at[0], recv_sem=recv_sem.at[index],
                device_id=sibling, device_id_type=MESH).wait_recv()

        sibling = at(0, k, 1)
        other = at(0, 1 - k, 0)
        partners = [sibling, other, at(1, 0, 0), at(1, 1, 0), at(-1, 0, 0), at(-1, 1, 0)]
        barrier = pltpu.get_barrier_semaphore()
        for partner in partners:
            pl.semaphore_signal(barrier, inc=1, device_id=partner, device_id_type=MESH)
        load_text = pltpu.make_async_copy(tx, tall.at[text(k)], load_sem.at[0])
        load_image = pltpu.make_async_copy(im, iall.at[pl.ds(0, rows)], load_sem.at[1])
        load_text.start()
        load_image.start()

        def logits(images, half, t, column):
            z[half * rows:(half + 1) * rows, column * rows:(column + 1) * rows] = scale * nt(
                images[half * rows:(half + 1) * rows, :], tall[text(t), :])

        def block(half, first, last):
            return z[half * rows:(half + 1) * rows, first * rows:last * rows]

        stat[...] = jnp.zeros_like(stat)
        load_text.wait()
        load_image.wait()
        logits(iall, 0, k, 0 if k == 0 else 3)
        pl.semaphore_wait(barrier, len(partners))

        def send_sib(p):
            send(im.at[piece(p)], iall.at[pl.ds(rows + p * part, part)], R_SIB + p, sibling)

        if k == 0:
            for p in range(PARTS):
                send(tx.at[piece(p)], tall.at[pl.ds(2 * rows + p * part, part)], R_T2 + p, at(-1, 0, 0))
            send(tx, tall.at[text(0)], R_T0, other)
            for p in range(PARTS):
                send_sib(p)
            arrived(tall.at[text(1)], R_T0)
            logits(iall, 0, 1, 1)
            for p in range(PARTS):
                piece_ref = tall.at[pl.ds(2 * rows + p * part, part)]
                arrived(piece_ref, R_T2 + p)
                send(piece_ref, piece_ref, R_T2 + p, other)
            logits(iall, 0, 2, 2)
            row_0 = lse_along(block(0, 0, 3))
            for p in range(PARTS):
                arrived(iall.at[pl.ds(rows + p * part, part)], R_SIB + p)
            for t in range(3):
                logits(iall, 1, t, t)
            for t in range(3):
                stat[t:t + 1, :] = lse_down(z[:, t * rows:(t + 1) * rows])
            row_1 = lse_along(block(1, 0, 3))
            for p in range(PARTS):
                arrived(tall.at[pl.ds(3 * rows + p * part, part)], R_T3 + p)
            for half in range(2):
                logits(iall, half, 3, 3)
            stat[3:4, :] = lse_down(z[:, 3 * rows:])
            stat[4:5, :] = joined(row_0, lse_along(block(0, 3, 4)))
            stat[5:6, :] = joined(row_1, lse_along(block(1, 3, 4)))
        else:
            def send_t3(p):
                send(tx.at[piece(p)], tall.at[pl.ds(3 * rows + p * part, part)], R_T3 + p, at(-1, 0, 0))

            for p in range(PARTS):
                send_sib(p)
            send(im, iprev.at[pl.ds(0, rows)], R_P0, at(1, 1, 0))
            send(tx, tall.at[text(1)], R_T0, other)
            send_t3(0)
            for p in range(PARTS):
                piece_ref = iall.at[pl.ds(rows + p * part, part)]
                arrived(piece_ref, R_SIB + p)
                send(piece_ref, iprev.at[pl.ds(rows + p * part, part)], R_P1 + p, at(1, 1, 0))
                if p + 1 < PARTS:
                    send_t3(p + 1)
            logits(iall, 1, 1, 3)
            for half in range(2):
                stat[4 + half:5 + half, :] = lse_along(block(half, 3, 4))
            col_a = lse_down(z[:, 3 * rows:])
            arrived(tall.at[text(0)], R_T0)
            arrived(iprev.at[pl.ds(0, rows)], R_P0)
            logits(iprev, 0, 0, 0)
            logits(iprev, 0, 1, 1)
            for p in range(PARTS):
                arrived(tall.at[pl.ds(2 * rows + p * part, part)], R_T2 + p)
            logits(iprev, 0, 2, 2)
            stat[6:7, :] = lse_along(block(0, 0, 3))
            col_b = [lse_down(block(0, t, t + 1)) for t in range(3)]
            col_b[1] = joined(col_b[1], col_a)
            for p in range(PARTS):
                arrived(iprev.at[pl.ds(rows + p * part, part)], R_P1 + p)
            for t in range(3):
                logits(iprev, 1, t, t)
            stat[7:8, :] = lse_along(block(1, 0, 3))
            for t in range(3):
                stat[t:t + 1, :] = joined(col_b[t], lse_down(block(1, t, t + 1)))

        if k == 1:
            send(stat, stats.at[S_PREV_X], R_STAT + S_PREV_X, at(1, 1, 1))
            send(stat, stats.at[S_NEXT_X], R_STAT + S_NEXT_X, at(-1, 1, 1))
        send(stat, stats.at[S_PREV + k], R_STAT + S_PREV + k, at(1, 1, 0))
        send(stat, stats.at[S_PREV + k], R_STAT + S_PREV + k, at(1, 0, 0))
        send(stat, stats.at[S_NEXT + k], R_STAT + S_NEXT + k, at(-1, 1, 0))
        send(stat, stats.at[S_NEXT + k], R_STAT + S_NEXT + k, at(-1, 0, 0))
        send(stat, stats.at[S_SIB], R_STAT + S_SIB, sibling)
        send(stat, stats.at[S_OTHER], R_STAT + S_OTHER, other)
        for slot in range(6 if k == 0 else 8):
            arrived(stats.at[slot], R_STAT + slot)

        def line(slot, row):
            return stats[slot, row:row + 1, :]

        def mine(row):
            return stat[row:row + 1, :]

        col = [
            joined(mine(0), line(S_OTHER, 0), line(S_PREV, 2), line(S_PREV + 1, 2)),
            joined(mine(1), line(S_OTHER, 1), line(S_PREV, 3)),
            joined(mine(2), line(S_OTHER, 2), line(S_NEXT, 0), line(S_NEXT + 1, 0)),
        ]
        if k == 0:
            col.append(joined(mine(3), line(S_NEXT, 1), line(S_NEXT + 1, 1)))
            row_a = [upright(joined(mine(4 + h), line(S_SIB, 5 - h))) for h in range(2)]
        else:
            row_a = [
                upright(joined(mine(4 + h), line(S_SIB, 5 - h), line(S_NEXT + 1, 6 + h), line(S_NEXT_X, 7 - h)))
                for h in range(2)]
            row_b = [
                upright(joined(mine(6 + h), line(S_SIB, 7 - h), line(S_PREV + 1, 4 + h), line(S_PREV_X, 5 - h)))
                for h in range(2)]

        def weigh(half, column, row_lse, col_lse, diagonal):
            at_rows = slice(half * rows, (half + 1) * rows)
            at_cols = slice(column * rows, (column + 1) * rows)
            block = z[at_rows, at_cols]
            weight = jnp.exp(block - row_lse) + jnp.exp(block - col_lse)
            if diagonal:
                i = lax.broadcasted_iota(jnp.int32, (rows, rows), 0)
                j = lax.broadcasted_iota(jnp.int32, (rows, rows), 1)
                weight = weight - 2.0 * (i == j).astype(jnp.float32)
            w[at_rows, at_cols] = (0.5 * scale * weight).astype(jnp.bfloat16)

        def columns(column):
            return slice(column * rows, (column + 1) * rows)

        b16 = jnp.bfloat16
        f32 = jnp.float32
        if k == 0:
            for t in range(4):
                weigh(1, t, row_a[1], col[t], False)
            stage[2] = nn(w[sib, :], tall[...]).astype(b16)
            for p in range(GPARTS):
                send(stage.at[2, gpiece(p)], gsib.at[gpiece(p)], R_GSIB + p, sibling)
            weigh(0, 3, row_a[0], col[3], False)
            stage[0] = tn(w[:, columns(3)], iall[...]).astype(b16)
            send(stage.at[0], gtx, R_GTX, at(1, 1, 0))
            weigh(0, 2, row_a[0], col[2], False)
            part_2 = tn(w[:, columns(2)], iall[...])
            arrived(gt2, R_GT2)
            stage[1] = (part_2 + gt2[...].astype(f32)).astype(b16)
            send(stage.at[1], gtx, R_GTX, at(1, 0, 0))
            for t in range(2):
                weigh(0, t, row_a[0], col[t], t == 0)
            stage[3] = tn(w[:, columns(1)], iall[...]).astype(b16)
            send(stage.at[3], gt0, R_GT0, other)
            tg[...] = tn(w[:, columns(0)], iall[...])
            pg[...] = nn(w[own, :], tall[...])
            arrived(gt0, R_GT0)
            tg[...] += gt0[...].astype(f32)
            for p in range(GPARTS):
                arrived(gsib.at[gpiece(p)], R_GSIB + p)
            arrived(gtx, R_GTX)
        else:
            for t in range(3):
                weigh(1, t, row_b[1], col[t], False)
            stage[2] = nn(w[sib, :3 * rows], tall[pl.ds(0, 3 * rows), :]).astype(b16)
            first = len(sent)
            for p in range(GPARTS):
                send(stage.at[2, gpiece(p)], gb.at[1, gpiece(p)], R_GB + GPARTS + p, at(-1, 1, 0))
            weigh(0, 2, row_b[0], col[2], False)
            stage[0] = tn(w[:, columns(2)], iprev[...]).astype(b16)
            send(stage.at[0], gt2, R_GT2, other)
            for t in range(2):
                weigh(0, t, row_b[0], col[t], False)
            stage[1] = nn(w[own, :3 * rows], tall[pl.ds(0, 3 * rows), :]).astype(b16)
            stage[3] = tn(w[:, columns(0)], iprev[...]).astype(b16)
            send(stage.at[3], gt0, R_GT0, other)
            for half in range(2):
                weigh(half, 3, row_a[half], col[1], half == 0)
            pg[...] = nn(w[sib, columns(3)], tall[text(1), :])
            tg[...] = tn(w[:, columns(1)], iprev[...]) + tn(w[:, columns(3)], iall[...])
            sent_early.extend(range(first, first + GPARTS))
            for p in range(GPARTS):
                sent[first + p].wait_send()
                send(stage.at[1, gpiece(p)], gb.at[0, gpiece(p)], R_GB + p, at(-1, 1, 0))
                arrived(gb.at[1, gpiece(p)], R_GB + GPARTS + p)
                stage[4, gpiece(p), :] = (pg[gpiece(p), :] + gb[1, gpiece(p), :].astype(f32)).astype(b16)
                send(stage.at[4, gpiece(p)], gsib.at[gpiece(p)], R_GSIB + p, sibling)
            pg[...] = nn(w[own, columns(3)], tall[text(1), :])
            arrived(gt0, R_GT0)
            tg[...] += gt0[...].astype(f32)
            for p in range(GPARTS):
                arrived(gb.at[0, gpiece(p)], R_GB + p)
                pg[gpiece(p), :] += gb[0, gpiece(p), :].astype(f32)
            arrived(gtx, R_GTX)
            for p in range(GPARTS):
                arrived(gsib.at[gpiece(p)], R_GSIB + p)
        for index, copy in enumerate(sent):
            if index not in sent_early:
                copy.wait_send()

    @pl.when(core == 0)
    def _():
        run(0)

    @pl.when(core == 1)
    def _():
        run(1)


def local(photo_vectors, caption_vectors, inverse_heat_factor):
    rows, depth = photo_vectors.shape
    n_dp = lax.axis_size("dp")
    vmem = pl.BlockSpec(memory_space=pltpu.VMEM)
    bf16 = jnp.bfloat16
    block = pltpu.VMEM((rows, depth), bf16)

    def body(*refs):
        kernel(n_dp, *refs)

    hbm = pl.BlockSpec(memory_space=pltpu.HBM)
    pg, tg, gsib, gtx = pl.pallas_call(
        body,
        out_shape=[jax.ShapeDtypeStruct((rows, depth), jnp.float32)] * 2
        + [jax.ShapeDtypeStruct((rows, depth), bf16)] * 2,
        in_specs=[pl.BlockSpec(memory_space=pltpu.SMEM), hbm, hbm],
        out_specs=[vmem] * 4,
        scratch_shapes=[
            pltpu.VMEM((2 * rows, depth), bf16),
            pltpu.VMEM((2 * rows, depth), bf16),
            pltpu.VMEM((4 * rows, depth), bf16),
            pltpu.VMEM((2 * rows, 4 * rows), jnp.float32),
            pltpu.VMEM((2 * rows, 4 * rows), bf16),
            pltpu.VMEM((8, rows), jnp.float32),
            pltpu.VMEM((8, 8, rows), jnp.float32),
            pltpu.VMEM((5, rows, depth), bf16),
            block,
            block,
            pltpu.VMEM((2, rows, depth), bf16),
            pltpu.SemaphoreType.DMA((64,)),
            pltpu.SemaphoreType.DMA((N_SEM,)),
            pltpu.SemaphoreType.DMA((2,)),
        ],
        compiler_params=pltpu.CompilerParams(
            collective_id=0, has_side_effects=True, vmem_limit_bytes=48 * 2**20),
        cost_estimate=pl.CostEstimate(
            flops=6 * 2 * rows * 4 * rows * depth, bytes_accessed=12 * rows * depth,
            transcendentals=4 * 8 * rows * rows),
        name="banded",
    )(inverse_heat_factor, pltpu.with_memory_space_constraint(photo_vectors, pltpu.HBM), pltpu.with_memory_space_constraint(caption_vectors, pltpu.HBM))
    return pg + gsib.astype(jnp.float32), tg + gtx.astype(jnp.float32)


def solution(mesh):
    in_specs = (P(("dp", "sub"), None), P(("dp", "sub"), None), P())
    out_specs = (P(("dp", "sub"), None), P(("dp", "sub"), None))
    return jax.shard_map(local, mesh=mesh, in_specs=in_specs, out_specs=out_specs, check_vma=False)
```
